32 devices in a mesh: seq: 4 (over x, core), head: 8 (over z, y).
Axes of the slice: x: 2, y: 2, z: 4, core: 2. Of those that a mesh axis runs over, the one named last changes fastest.
Arguments:
- moe_input: bfloat16 [4096, 1536], P(('seq', 'head')), may hold values from -6 to 6
- out_grad: bfloat16 [4096, 1536], P(('seq', 'head')), may hold values from -6 to 6
- route_ids: int32 [4096, 6], P(('seq', 'head')), may hold values from 0 to 63, all different within a row; in each aligned block of 128 rows (0 to 127, 128 to 255, ...) at most 16 rows name the same one
- route_gates: float32 [4096, 6], P(('seq', 'head')), may hold values from 0.05 to 0.35
- gate_halves: bfloat16 [128, 1536, 256], P(('seq', 'head')), may hold values from -0.15625 to 0.15625
- up_halves: bfloat16 [128, 1536, 256], P(('seq', 'head')), may hold values from -0.15625 to 0.15625
- down_halves: bfloat16 [128, 256, 1536], P(('seq', 'head')), may hold values from -0.25 to 0.25
- out_proj: bfloat16 [3072, 1536], P('head'), may hold values from -0.109375 to 0.109375
- ssd_x: float32 [4096, 3072], P('seq', 'head'), may hold values from -0.125 to 0.125
- b_proj: float32 [4096, 128], P('seq'), may hold values from -0.5 to 0.5
- c_proj: float32 [4096, 128], P('seq'), may hold values from -0.5 to 0.5
- log_decay: float32 [48, 4096], P('head', 'seq'), may hold values from -2.3 to 0, as said below
- skip_gain: float32 [48], P('head'), may hold values from 0.5 to 1.5
Outputs:
- resid_grad: bfloat16 [4096, 1536], P(('seq', 'head'))
- ssd_x_grad: float32 [4096, 3072], P('seq', 'head')
- b_grad: float32 [4096, 128], P(('seq', 'head'))
The draws below stay inside these ranges and needn't reach their ends.
Inputs may be any that keep to these rules, and one draw needn't show every extreme that they name: `route_ids`: each row names 6 different experts; the 128 rows of one device name any one expert at most 16 times, a bound that some block reaches. `log_decay`: negative.
All inputs are finite; a program needn't handle non-finite values.
Results may differ from the reference program's by a relative error of at most 0.0039.
Values may be sent and summed in bfloat16 or wider, within the bound.
A program may use at most 128 MiB of HBM per device.

```python
import math
import jax
import jax.numpy as jnp
import numpy as np
from jax import lax

D = 1536
EXPERTS = 64
TOPK = 6
FFE = 512
SCAN_HEADS = 48
HEAD_DIM = 64
STATE = 128
BLOCK = 256
TOK_DEV = 128
HALF = 256
CAP = 16
SEQUENCE_TOKENS = 4096
N_SEQ = 4
N_HEAD = 8


def draw_log_decay(key, part):
    pick_key, fast_key, slow_key, span_key, rough_key, where_key, spike_depth_key = jax.random.split(key, 7)
    fast_share = 0.5
    is_fast = jax.random.uniform(pick_key, (SCAN_HEADS,), jnp.float32) < fast_share
    fast_rate = jnp.exp(jax.random.uniform(fast_key, (SCAN_HEADS,), jnp.float32, math.log(1.0 / 50.0), math.log(1.0 / 30.0)))
    slow_rate = jnp.exp(jax.random.uniform(slow_key, (SCAN_HEADS,), jnp.float32, math.log(0.1), math.log(0.8))) / SEQUENCE_TOKENS
    baseline_decay_rate = jnp.where(is_fast, fast_rate, slow_rate)
    span_count = SEQUENCE_TOKENS // BLOCK
    spread_multiplier = jnp.exp(jax.random.uniform(span_key, (SCAN_HEADS, span_count, 1), jnp.float32, math.log(0.5), math.log(2.0)))
    spread_multiplier = jnp.broadcast_to(spread_multiplier, (SCAN_HEADS, span_count, BLOCK)).reshape(SCAN_HEADS, SEQUENCE_TOKENS)
    jitter_level = jnp.exp(jax.random.uniform(rough_key, (SCAN_HEADS, SEQUENCE_TOKENS), jnp.float32, math.log(0.5), math.log(2.0)))
    spike_positions = jax.random.randint(where_key, (3,), 0, SEQUENCE_TOKENS)
    spike_depth = jax.random.uniform(spike_depth_key, (3, SCAN_HEADS), jnp.float32, 0.22, 0.69)
    spike_count = (jnp.arange(SEQUENCE_TOKENS, dtype=jnp.int32)[None, :] == spike_positions[:, None]).astype(jnp.float32)
    spike_events = jnp.einsum('dq,dc->qc', spike_depth, spike_count)
    return -(baseline_decay_rate[:, None] * spread_multiplier * jitter_level) - spike_events


def block_scale(own_key, dims, pieces, smallest, top_value):
    level, own = 1.0, jax.random.fold_in(own_key, 6)
    for dim, shards_of in pieces:
        heights = jnp.exp(jax.random.uniform(jax.random.fold_in(own, dim), (shards_of,), jnp.float32, smallest / len(pieces), top_value / len(pieces)))
        level = level * jnp.repeat(heights, dims[dim] // shards_of).reshape([-1 if axis == dim else 1 for axis in range(len(dims))])
    return level


def assign_block(stream_key, own, number, rows, amount, top, reach, lean):
    sequence = jax.random.permutation(stream_key, amount)
    crowded, ordinary = portions_of(amount, rows * top, reach, lean, True), portions_of(amount, rows * top, reach, lean, False)
    places = jnp.arange(amount)

    def named(lengths, offset_by):
        used = int((lengths > 0).sum())
        fixed = max(1, used // 4)
        passed = fixed + (places - fixed + offset_by * (used - fixed)) % max(1, amount - fixed)
        return jnp.zeros((amount,), jnp.int32).at[sequence[jnp.where(places < fixed, places, passed)]].set(jnp.asarray(lengths, jnp.int32))

    lengths = jnp.where(number % 4 == 0, named(crowded, number // 4), named(ordinary, number - number // 4 - 1))
    mixed = jax.random.permutation(jax.random.fold_in(own, 3), amount)
    source_of, sink = mixed[0:amount // 2 * 2:2], mixed[1:amount // 2 * 2:2]
    slack = jnp.minimum(lengths[source_of] - 1, reach - lengths[sink]) // 2
    slack = jnp.where((source_of == sequence[0]) | (sink == sequence[0]) | (lengths[sink] == 0), 0, jnp.maximum(slack, 0))
    passed = jax.random.randint(jax.random.fold_in(own, 4), (amount // 2,), 0, 1 << 20) % (slack + 1)
    lengths = lengths.at[source_of].add(-passed).at[sink].add(passed)
    members = jnp.searchsorted(jnp.cumsum(lengths), jnp.arange(rows * top), side="right").astype(jnp.int32)
    listing = members.reshape(top, rows).T
    listing = listing[jax.random.permutation(jax.random.fold_in(own, 1), rows)]
    offset_by = jax.random.randint(jax.random.fold_in(own, 2), (rows, 1), 0, top)
    return jnp.take_along_axis(listing, (jnp.arange(top)[None, :] + offset_by) % top, axis=1)


def portions_of(count, total, limit, slope, full):
    weights = [(1 << 20) // math.isqrt(rank ** slope) + 1 for rank in range(1, count + 1)]
    largest = limit if full else min(limit, max(-(-total // count), total * weights[0] // sum(weights)))
    least = 1 if total - largest >= count - 1 else 0
    holding, surplus = [largest] + [least] * (count - 1), total - largest - least * (count - 1)
    while surplus > 0:
        movable = [i for i in range(1, count) if holding[i] < largest] or [i for i in range(1, count) if holding[i] < limit]
        mass, remaining = sum([weights[i] for i in movable]), surplus
        for i in movable:
            more = min(limit - holding[i], max(1, remaining * weights[i] // mass), surplus)
            holding[i] = holding[i] + more
            surplus = surplus - more
    return np.array(holding)


def gaussian(stream_key, extent, deviation, reach, cuts=(), held_as=jnp.bfloat16):
    values = deviation * jax.random.normal(stream_key, extent, jnp.float32)
    if cuts:
        values = values * block_scale(stream_key, extent, cuts, -0.22, 0.18)
    return jnp.clip(values, -reach, reach).astype(held_as)


def setup_inputs(seed: int = 0) -> dict:
    splits = jax.random.split(jax.random.key(seed), 14)
    moe_input = gaussian(splits[0], (SEQUENCE_TOKENS, D), 1.0, 6.0, ((0, 32),))
    out_grad = gaussian(splits[1], (SEQUENCE_TOKENS, D), 1.0, 6.0, ((0, 32),))
    route_ids_keys = jax.random.split(jax.random.fold_in(splits[2], 1), SEQUENCE_TOKENS // TOK_DEV)
    route_ids_turns = jax.random.permutation(jax.random.fold_in(splits[2], 3), SEQUENCE_TOKENS // TOK_DEV)
    route_ids = jax.vmap(lambda own, number: assign_block(jax.random.fold_in(splits[2], 2), own, number, TOK_DEV, EXPERTS, TOPK, CAP, 2))(route_ids_keys, route_ids_turns).reshape((SEQUENCE_TOKENS, TOPK))
    route_gates = jnp.clip(0.05 + 0.29999999 * jax.random.uniform(splits[3], (SEQUENCE_TOKENS, TOPK), jnp.float32) ** block_scale(splits[3], (SEQUENCE_TOKENS, TOPK), ((0, 32),), -0.2, 0.2), 0.05, 0.35)
    gate_halves = gaussian(splits[4], (2 * EXPERTS, D, HALF), D ** -0.5, 0.15625, ((0, 32),))
    up_halves = gaussian(splits[5], (2 * EXPERTS, D, HALF), D ** -0.5, 0.15625, ((0, 32),))
    down_halves = gaussian(splits[6], (2 * EXPERTS, HALF, D), FFE ** -0.5, 0.25, ((0, 32),))
    out_proj = gaussian(splits[7], (SCAN_HEADS * HEAD_DIM, D), (SCAN_HEADS * HEAD_DIM) ** -0.5, 0.109375, ((0, 8),))
    ssd_x = gaussian(splits[8], (SEQUENCE_TOKENS, SCAN_HEADS * HEAD_DIM), 0.02, 0.125, ((0, 4), (1, 8)), jnp.float32)
    b_proj = gaussian(splits[9], (SEQUENCE_TOKENS, STATE), 0.09, 0.5, ((0, 4),), jnp.float32)
    c_proj = gaussian(splits[10], (SEQUENCE_TOKENS, STATE), 0.09, 0.5, ((0, 4),), jnp.float32)
    log_decay = draw_log_decay(jax.random.fold_in(splits[13], 71), 0)
    skip_gain = jnp.clip(0.5 + 1.0 * jax.random.uniform(splits[12], (SCAN_HEADS,), jnp.float32) ** block_scale(splits[12], (SCAN_HEADS,), ((0, 8),), -0.2, 0.2), 0.5, 1.5)
    return dict(moe_input=moe_input, out_grad=out_grad, route_ids=route_ids, route_gates=route_gates, gate_halves=gate_halves, up_halves=up_halves, down_halves=down_halves, out_proj=out_proj, ssd_x=ssd_x, b_proj=b_proj, c_proj=c_proj, log_decay=log_decay, skip_gain=skip_gain)


def reference(moe_input, out_grad, route_ids, route_gates, gate_halves, up_halves, down_halves, out_proj, ssd_x, b_proj, c_proj, log_decay, skip_gain):
    highest = lax.Precision.HIGHEST
    flat_ids = route_ids.reshape(-1)
    flat_gates = route_gates.reshape(-1)
    row_limit = N_SEQ * N_HEAD * CAP
    gate_full = gate_halves.reshape(EXPERTS, 2, D, HALF).transpose(0, 2, 1, 3).reshape(EXPERTS, D, FFE)
    up_full = up_halves.reshape(EXPERTS, 2, D, HALF).transpose(0, 2, 1, 3).reshape(EXPERTS, D, FFE)
    down_full = down_halves.reshape(EXPERTS, FFE, D)

    def one_expert(accumulated, expert):
        key_rank = jnp.where(flat_ids == expert, 0, 1).astype(jnp.int32)
        order = jnp.argsort(key_rank, stable=True)[:row_limit]
        matched = flat_ids[order] == expert
        token_index = (order // TOPK).astype(jnp.int32)
        zero_row = jnp.zeros((), moe_input.dtype)
        rows_in = jnp.where(matched[:, None], moe_input[token_index], zero_row)
        rows_grad = jnp.where(matched[:, None], out_grad[token_index], zero_row)
        gate_act = jnp.dot(rows_in, gate_full[expert], preferred_element_type=jnp.float32)
        up_act = jnp.dot(rows_in, up_full[expert], preferred_element_type=jnp.float32)
        hidden_grad = jnp.dot(rows_grad, down_full[expert].T, preferred_element_type=jnp.float32)
        sigmoid_act = jax.nn.sigmoid(gate_act)
        gate_grad = (hidden_grad * up_act * sigmoid_act * (1.0 + gate_act * (1.0 - sigmoid_act))).astype(jnp.bfloat16)
        up_grad = (hidden_grad * gate_act * sigmoid_act).astype(jnp.bfloat16)
        route_term = jnp.dot(gate_grad, gate_full[expert].T, preferred_element_type=jnp.float32)
        route_term = route_term + jnp.dot(up_grad, up_full[expert].T, preferred_element_type=jnp.float32)
        route_term = lax.optimization_barrier(route_term.astype(jnp.bfloat16))
        weight = jnp.where(matched, flat_gates[order], 0.0)
        accumulated = accumulated.at[token_index].add(weight[:, None] * route_term.astype(jnp.float32))
        return accumulated, None

    accumulated, _ = lax.scan(one_expert, jnp.zeros((SEQUENCE_TOKENS, D), jnp.float32), jnp.arange(EXPERTS, dtype=jnp.int32))
    resid_grad = (out_grad.astype(jnp.float32) + accumulated).astype(jnp.bfloat16)
    ssd_grad = jnp.dot(resid_grad, out_proj.T, preferred_element_type=jnp.float32)

    block_count = SEQUENCE_TOKENS // BLOCK
    grad_blocks = ssd_grad.reshape(block_count, BLOCK, SCAN_HEADS, HEAD_DIM)
    input_blocks = ssd_x.reshape(block_count, BLOCK, SCAN_HEADS, HEAD_DIM)
    b_blocks = b_proj.reshape(block_count, BLOCK, STATE)
    c_blocks = c_proj.reshape(block_count, BLOCK, STATE)
    decay_blocks = log_decay.reshape(SCAN_HEADS, block_count, BLOCK).transpose(1, 0, 2)
    causal = jnp.arange(BLOCK)[:, None] >= jnp.arange(BLOCK)[None, :]

    def block_step(carry, blocks_in):
        grad_block, input_block, b_block, c_block, decay_block = blocks_in
        within = jnp.cumsum(decay_block, axis=1)
        log_gap = within[:, :, None] - within[:, None, :]
        scores = jnp.dot(c_block, b_block.T, precision=highest)
        weights = jnp.where(causal[None], jnp.exp(jnp.where(causal[None], log_gap, 0.0)), 0.0) * scores[None]
        to_end = jnp.exp(within[:, -1:] - within)
        grad_x = jnp.einsum("hts,thp->shp", weights, grad_block, precision=highest)
        grad_x = grad_x + jnp.einsum("hs,sn,hpn->shp", to_end, b_block, carry, precision=highest)
        grad_x = grad_x + skip_gain[None, :, None] * grad_block
        inner_prod = jnp.einsum("thp,shp->hts", grad_block, input_block, precision=highest)
        grad_b = jnp.einsum("hts,tn->sn", weights * inner_prod, c_block, precision=highest)
        grad_b = grad_b + jnp.einsum("hs,shp,hpn->sn", to_end, input_block, carry, precision=highest)
        carry = jnp.exp(within[:, -1])[:, None, None] * carry + jnp.einsum("ht,thp,tn->hpn", jnp.exp(within), grad_block, c_block, precision=highest)
        return carry, (grad_x, grad_b)

    zero_state = jnp.zeros((SCAN_HEADS, HEAD_DIM, STATE), jnp.float32)
    _, (grad_x, grad_b) = lax.scan(block_step, zero_state, (grad_blocks, input_blocks, b_blocks, c_blocks, decay_blocks), reverse=True)
    return resid_grad, grad_x.reshape(SEQUENCE_TOKENS, SCAN_HEADS * HEAD_DIM), grad_b.reshape(SEQUENCE_TOKENS, STATE)
```

```python
import functools
import jax
import jax.numpy as jnp
from jax import lax
from jax.experimental import pallas as pl
from jax.experimental.pallas import tpu as pltpu
from jax.sharding import PartitionSpec as P

BLOCK = 256
DEVICES = ("seq", "head")


def from_partner(shard, axis, distance):
    return lax.ppermute(shard, axis, [(i, i ^ 1 << distance) for i in range(lax.axis_size(axis))])


def expert_kernel(x_ref, g_ref, gate_ref, up_ref, down_ref, out_ref):
    last = (((1,), (1,)), ((), ()))
    f32 = jnp.float32
    x, g = x_ref[...], g_ref[...]
    total = None
    for j in range(gate_ref.shape[0]):
        gate_act = jnp.dot(x, gate_ref[j], preferred_element_type=f32)
        up_act = jnp.dot(x, up_ref[j], preferred_element_type=f32)
        hidden_grad = lax.dot_general(g, down_ref[j], last, preferred_element_type=f32)
        s = jax.nn.sigmoid(gate_act)
        gate_grad = (hidden_grad * up_act * s * (1.0 + gate_act * (1.0 - s))).astype(jnp.bfloat16)
        up_grad = (hidden_grad * gate_act * s).astype(jnp.bfloat16)
        term = lax.dot_general(gate_grad, gate_ref[j], last, preferred_element_type=f32)
        term = term + lax.dot_general(up_grad, up_ref[j], last, preferred_element_type=f32)
        total = term if total is None else total + term
    out_ref[...] = total.astype(out_ref.dtype)


def swiglu_back(rows_in, rows_grad, gate, up, down):
    rows, width = rows_in.shape
    halves, _, hidden = gate.shape
    tile = 256 if rows % 256 == 0 else rows
    row = pl.BlockSpec((tile, width), lambda i: (i, 0))
    return pl.pallas_call(
        expert_kernel,
        grid=(rows // tile,),
        in_specs=[
            row,
            row,
            pl.BlockSpec(gate.shape, lambda i: (0, 0, 0)),
            pl.BlockSpec(up.shape, lambda i: (0, 0, 0)),
            pl.BlockSpec(down.shape, lambda i: (0, 0, 0)),
        ],
        out_specs=row,
        out_shape=jax.ShapeDtypeStruct((rows, width), jnp.bfloat16),
        compiler_params=pltpu.CompilerParams(vmem_limit_bytes=48 * 1024 * 1024),
        cost_estimate=pl.CostEstimate(
            flops=10 * rows * width * halves * hidden,
            bytes_accessed=6 * rows * width + 6 * halves * width * hidden,
            transcendentals=rows * halves * hidden,
        ),
    )(rows_in, rows_grad, gate, up, down)


def split_bf16(a):
    high = a.astype(jnp.bfloat16)
    return high, (a - high.astype(jnp.float32)).astype(jnp.bfloat16)


def shards(
    moe_input,
    out_grad,
    route_ids,
    route_gates,
    gate_halves,
    up_halves,
    down_halves,
    out_proj,
    ssd_x,
    b_proj,
    c_proj,
    log_decay,
    skip_gain,
):
    highest = lax.Precision.HIGHEST
    tok_rows, feature_width = moe_input.shape
    top_count = route_ids.shape[1]
    devices = lax.axis_size(("seq", "head"))
    halves_dev = gate_halves.shape[0]
    experts = devices * halves_dev // 2
    capacity = tok_rows // 8
    expert_ids = jnp.arange(experts, dtype=jnp.int32)
    chosen = route_ids[:, :, None] == expert_ids[None, None, :]
    member = jnp.any(chosen, axis=1)
    gate_of = jnp.sum(jnp.where(chosen, route_gates[:, :, None], 0.0), axis=1)
    token = jnp.arange(tok_rows)
    earlier = (token[:, None] > token[None, :]).astype(jnp.bfloat16)
    rank = jnp.dot(earlier, member.astype(jnp.bfloat16), preferred_element_type=jnp.float32)
    rank = jnp.where(member, rank, -1.0)
    half_width = gate_halves.shape[2]
    if halves_dev == 1:
        parity = lax.axis_index(("seq", "head")) % 2
        other_gate, other_up, other_down = from_partner(
            (gate_halves, up_halves, down_halves), ("seq", "head"), 0
        )
        first_side = parity == 0
        stack = lambda own, other: jnp.where(
            first_side, jnp.stack([own, other], 1), jnp.stack([other, own], 1)
        )
        gate_w, up_w, down_w = (
            stack(gate_halves, other_gate),
            stack(up_halves, other_up),
            stack(down_halves, other_down),
        )
        items_dev = 1
    else:
        items_dev = halves_dev // 2
        gate_w = gate_halves.reshape(items_dev, 2, feature_width, half_width)
        up_w = up_halves.reshape(items_dev, 2, feature_width, half_width)
        down_w = down_halves.reshape(items_dev, 2, half_width, feature_width)
    slot_count = experts * capacity // (devices * items_dev)
    f32 = jnp.float32
    exchange = functools.partial(
        lax.all_to_all, axis_name=DEVICES, split_axis=0, concat_axis=0, tiled=True
    )
    moe_grad = out_grad.astype(f32)
    for item in range(items_dev):
        slot = (
            jnp.arange(devices)[:, None] * (items_dev * slot_count)
            + item * slot_count
            + jnp.arange(slot_count)[None, :]
        ).reshape(-1)
        slot_expert = (slot // capacity).astype(jnp.int32)
        pick = (expert_ids[:, None] == slot_expert[None, :]).astype(f32)
        slot_rank = jnp.dot(rank.astype(jnp.bfloat16), pick.astype(jnp.bfloat16), preferred_element_type=f32)
        here = slot_rank == (slot % capacity).astype(f32)[None, :]
        slot_gate = jnp.where(here, jnp.dot(gate_of, pick, precision=highest), 0.0)
        take = here.T.astype(jnp.bfloat16)
        send_input = jnp.dot(take, moe_input, preferred_element_type=jnp.bfloat16)
        send_grad = jnp.dot(take, out_grad, preferred_element_type=jnp.bfloat16)
        recv_input = exchange(send_input)
        recv_grad = exchange(send_grad)
        terms = swiglu_back(recv_input, recv_grad, gate_w[item], up_w[item], down_w[item])
        returned = exchange(terms)
        high, low = split_bf16(slot_gate)
        moe_grad = moe_grad + jnp.dot(high, returned, preferred_element_type=f32)
        moe_grad = moe_grad + jnp.dot(low, returned, preferred_element_type=f32)
    resid_grad = moe_grad.astype(jnp.bfloat16)
    inner_dev = out_proj.shape[0]
    heads_dev = skip_gain.shape[0]
    head_dim = inner_dev // heads_dev
    seq_rows, state_dim = b_proj.shape
    block_len = BLOCK
    block_count = seq_rows // block_len
    decay = log_decay.reshape(heads_dev, block_count, block_len)
    causal = jnp.arange(block_len)[:, None] >= jnp.arange(block_len)[None, :]
    within = jnp.einsum("hbr,tr->hbt", decay, causal.astype(f32), precision=highest)
    block_sum = within[:, :, -1]
    later_sum = [jnp.zeros((heads_dev,), f32)]
    for block in reversed(range(1, block_count)):
        later_sum.insert(0, later_sum[0] + block_sum[:, block])
    tail = jnp.stack(later_sum, 1)
    total = later_sum[0] + block_sum[:, 0]
    totals = lax.all_gather(total, "seq")
    seq_count, place = lax.axis_size("seq"), lax.axis_index("seq")
    between = jnp.zeros((heads_dev,), f32)
    carried = []
    for source in range(seq_count):
        carried.append(jnp.where(source > place, jnp.exp(between), 0.0))
        between = between + jnp.where(source > place, totals[source], 0.0)
    b_blocks = b_proj.reshape(block_count, block_len, state_dim)
    c_blocks = c_proj.reshape(block_count, block_len, state_dim)
    x_blocks = ssd_x.reshape(block_count, block_len, heads_dev, head_dim)
    scores = jnp.einsum("btn,bsn->bts", c_blocks, b_blocks, precision=highest)
    log_gap = within[:, :, :, None] - within[:, :, None, :]
    weights = jnp.where(causal, jnp.exp(jnp.where(causal, log_gap, 0.0)), 0.0) * scores[None]
    to_start = jnp.exp(within)
    to_end = jnp.exp(block_sum[:, :, None] - within)
    block_decay = jnp.exp(block_sum)
    ssd_grad = jnp.einsum(
        "td,kd->tk",
        lax.all_gather(resid_grad, "head", axis=0, tiled=True),
        out_proj,
        preferred_element_type=jnp.float32,
    )
    g_blocks = ssd_grad.reshape(block_count, block_len, heads_dev, head_dim)
    intra_x = jnp.einsum("hbts,bthp->bshp", weights, g_blocks, precision=highest)
    inner_prod = jnp.einsum("bthp,bshp->hbts", g_blocks, x_blocks, precision=highest)
    intra_b = jnp.einsum("hbts,btn->bsn", weights * inner_prod, c_blocks, precision=highest)
    block_state = jnp.einsum("hbt,bthp,btn->bhpn", to_start, g_blocks, c_blocks, precision=highest)

    carry = jnp.zeros((heads_dev, head_dim, state_dim), f32)
    after = []
    for block in reversed(range(block_count)):
        after.insert(0, carry)
        carry = block_decay[:, block, None, None] * carry + block_state[block]
    states = lax.all_gather(carry, "seq")
    incoming = sum(carried[s][:, None, None] * states[s] for s in range(seq_count))
    future = jnp.stack(after) + jnp.exp(tail).T[:, :, None, None] * incoming[None]
    cross_x = jnp.einsum("hbs,bsn,bhpn->bshp", to_end, b_blocks, future, precision=highest)
    grad_x = intra_x + cross_x + skip_gain[None, None, :, None] * g_blocks
    cross_b = jnp.einsum("hbs,bshp,bhpn->bsn", to_end, x_blocks, future, precision=highest)
    partial_b = (intra_b + cross_b).reshape(seq_rows, state_dim)
    parts = lax.all_to_all(partial_b, "head", split_axis=0, concat_axis=0, tiled=True)
    b_grad = jnp.sum(parts.reshape(lax.axis_size("head"), -1, state_dim), axis=0)
    return (resid_grad, grad_x.reshape(seq_rows, inner_dev), b_grad)


def solution(mesh):
    return jax.shard_map(
        shards,
        mesh=mesh,
        in_specs=(
            P(("seq", "head"), None),
            P(("seq", "head"), None),
            P(("seq", "head"), None),
            P(("seq", "head"), None),
            P(("seq", "head"), None, None),
            P(("seq", "head"), None, None),
            P(("seq", "head"), None, None),
            P("head", None),
            P("seq", "head"),
            P("seq", None),
            P("seq", None),
            P("head", "seq"),
            P("head"),
        ),
        out_specs=(P(("seq", "head"), None), P("seq", "head"), P(("seq", "head"), None)),
        check_vma=False,
    )
```

```python
import functools
import jax
import jax.numpy as jnp
from jax import lax
from jax.experimental import pallas as pl
from jax.experimental.pallas import tpu as pltpu
from jax.sharding import Mesh, PartitionSpec as P

BLOCK = 256
HEAD = ("z", "y")
DEVICES = ("seq", "z", "y")
PLANE = ("seq", "y")


def from_partner(shard, axis, distance):
    return lax.ppermute(shard, axis, [(i, i ^ 1 << distance) for i in range(lax.axis_size(axis))])


def expert_kernel(x_ref, g_ref, gate_ref, up_ref, down_ref, out_ref):
    last = (((1,), (1,)), ((), ()))
    f32 = jnp.float32
    x, g = x_ref[...], g_ref[...]
    total = None
    for j in range(gate_ref.shape[0]):
        gate_act = jnp.dot(x, gate_ref[j], preferred_element_type=f32)
        up_act = jnp.dot(x, up_ref[j], preferred_element_type=f32)
        hidden_grad = lax.dot_general(g, down_ref[j], last, preferred_element_type=f32)
        s = jax.nn.sigmoid(gate_act)
        gate_grad = (hidden_grad * up_act * s * (1.0 + gate_act * (1.0 - s))).astype(jnp.bfloat16)
        up_grad = (hidden_grad * gate_act * s).astype(jnp.bfloat16)
        term = lax.dot_general(gate_grad, gate_ref[j], last, preferred_element_type=f32)
        term = term + lax.dot_general(up_grad, up_ref[j], last, preferred_element_type=f32)
        total = term if total is None else total + term
    out_ref[...] = total.astype(out_ref.dtype)


def swiglu_back(rows_in, rows_grad, gate, up, down):
    rows, width = rows_in.shape
    halves, _, hidden = gate.shape
    tile = 256 if rows % 256 == 0 else rows
    row = pl.BlockSpec((tile, width), lambda i: (i, 0))
    return pl.pallas_call(
        expert_kernel,
        grid=(rows // tile,),
        in_specs=[
            row,
            row,
            pl.BlockSpec(gate.shape, lambda i: (0, 0, 0)),
            pl.BlockSpec(up.shape, lambda i: (0, 0, 0)),
            pl.BlockSpec(down.shape, lambda i: (0, 0, 0)),
        ],
        out_specs=row,
        out_shape=jax.ShapeDtypeStruct((rows, width), jnp.bfloat16),
        compiler_params=pltpu.CompilerParams(vmem_limit_bytes=48 * 1024 * 1024),
        cost_estimate=pl.CostEstimate(
            flops=10 * rows * width * halves * hidden,
            bytes_accessed=6 * rows * width + 6 * halves * width * hidden,
            transcendentals=rows * halves * hidden,
        ),
    )(rows_in, rows_grad, gate, up, down)


def gather_kernel(count, z_size, y_size, *refs):
    own, out = refs[:count], refs[count : 2 * count]
    z_send, z_recv, y_send, y_recv, local_sem = refs[2 * count :]
    seq, z, y = (lax.axis_index(a) for a in DEVICES)
    mesh_ids = pl.DeviceIdType.MESH
    place = lambda block, column: block * y_size + column if y_size > 1 else block

    local = [
        pltpu.make_async_copy(own[i], out[i].at[place(z, y)], local_sem.at[i]) for i in range(count)
    ]
    for copy in local:
        copy.start()
    barrier = pltpu.get_barrier_semaphore()
    signals = 0
    for dz in range(z_size):
        for dy in range(y_size):
            if dz or dy:
                peer = (seq, lax.rem(z + dz, z_size), lax.rem(y + dy, y_size) if y_size > 1 else y)
                pl.semaphore_signal(barrier, inc=1, device_id=peer, device_id_type=mesh_ids)
                signals += 1
    pl.semaphore_wait(barrier, signals)
    for copy in local:
        copy.wait()

    def z_copy(i, way, step, block, target):
        ref = out[i].at[place(block, y)]
        return pltpu.make_async_remote_copy(
            src_ref=ref,
            dst_ref=ref,
            send_sem=z_send.at[i, way, step],
            recv_sem=z_recv.at[i, way, step],
            device_id=(seq, target, y),
            device_id_type=mesh_ids,
        )

    def y_copy(i, shift, way, step, block, column):
        ref = out[i].at[place(block, column)]
        return pltpu.make_async_remote_copy(
            src_ref=ref,
            dst_ref=ref,
            send_sem=y_send.at[i, shift - 1, way, step],
            recv_sem=y_recv.at[i, shift - 1, way, step],
            device_id=(seq, z, lax.rem(y + shift, y_size)),
            device_id_type=mesh_ids,
        )

    def within(index):
        return jnp.logical_and(index >= 0, index < z_size)

    ways = ((0, 1), (1, -1))

    def across(run, way, step, block, sending):
        for i in range(count):
            for shift in range(1, y_size):
                column = y if sending else lax.rem(y + y_size - shift, y_size)
                run(y_copy(i, shift, way, step, block, column))

    start = lambda c: c.start()
    wait_send = lambda c: c.wait_send()
    wait_recv = lambda c: c.wait_recv()
    for step in range(z_size - 1):
        for way, sign in ways:
            block = z - sign * step

            @pl.when(jnp.logical_and(within(block), within(z + sign)))
            def _():
                for i in range(count):
                    z_copy(i, way, step, block, z + sign).start()

        if step == 0:
            across(start, 0, 0, z, True)
        for way, sign in ways:
            arriving = z - sign * (step + 1)

            @pl.when(within(arriving))
            def _():
                for i in range(count):
                    z_copy(i, way, step, arriving, z).wait_recv()
                across(start, way, step + 1, arriving, True)

    if z_size == 1:
        across(start, 0, 0, z, True)
    across(wait_send, 0, 0, z, True)
    across(wait_recv, 0, 0, z, False)
    for step in range(z_size - 1):
        for way, sign in ways:
            block = z - sign * step
            arriving = z - sign * (step + 1)

            @pl.when(jnp.logical_and(within(block), within(z + sign)))
            def _():
                for i in range(count):
                    z_copy(i, way, step, block, z + sign).wait_send()

            @pl.when(within(arriving))
            def _():
                across(wait_send, way, step + 1, arriving, True)
                across(wait_recv, way, step + 1, arriving, False)


def gather(arrays, with_y, collective_id):
    z_size = lax.axis_size("z")
    y_size = lax.axis_size("y") if with_y else 1
    count = len(arrays)
    vmem = pl.BlockSpec(memory_space=pltpu.VMEM)
    dma = pltpu.SemaphoreType.DMA
    steps = max(1, z_size - 1)
    out = pl.pallas_call(
        functools.partial(gather_kernel, count, z_size, y_size),
        in_specs=[vmem] * count,
        out_specs=[vmem] * count,
        out_shape=[jax.ShapeDtypeStruct((z_size * y_size, *a.shape), a.dtype) for a in arrays],
        scratch_shapes=[
            dma((count, 2, steps)),
            dma((count, 2, steps)),
            dma((count, max(1, y_size - 1), 2, z_size)),
            dma((count, max(1, y_size - 1), 2, z_size)),
            dma((count,)),
        ],
        compiler_params=pltpu.CompilerParams(
            collective_id=collective_id,
            has_side_effects=True,
            vmem_limit_bytes=32 * 1024 * 1024,
        ),
    )(*arrays)
    return [a.reshape(-1, a.shape[-1]) for a in out]


def split_bf16(a):
    high = lax.reduce_precision(a, 8, 7).astype(jnp.bfloat16)
    return high, (a - high.astype(jnp.float32)).astype(jnp.bfloat16)


def shards(
    moe_input,
    out_grad,
    route_ids,
    route_gates,
    gate_halves,
    up_halves,
    down_halves,
    out_proj,
    ssd_x,
    b_proj,
    c_proj,
    log_decay,
    skip_gain,
):
    highest = lax.Precision.HIGHEST
    tok_rows, feature_width = moe_input.shape
    top_count = route_ids.shape[1]
    devices = lax.axis_size(DEVICES)
    halves_dev = gate_halves.shape[0]
    experts = devices * halves_dev // 2
    capacity = tok_rows // 8
    expert_ids = jnp.arange(experts, dtype=jnp.int32)
    z_size, y_size, z_place = lax.axis_size("z"), lax.axis_size("y"), lax.axis_index("z")
    meta = jnp.concatenate([route_ids.astype(jnp.float32), route_gates], axis=1)
    meta = jnp.pad(meta, ((0, 0), (0, -meta.shape[1] % 128)))
    line_input, line_grad, line_meta = gather([moe_input, out_grad, meta], False, 0)
    line_ids = line_meta[:, :top_count].astype(jnp.int32)
    line_gates = line_meta[:, top_count : 2 * top_count]
    chosen = line_ids[:, :, None] == expert_ids[None, None, :]
    member = jnp.any(chosen, axis=1)
    gate_of = jnp.sum(jnp.where(chosen, line_gates[:, :, None], 0.0), axis=1)
    token = jnp.arange(z_size * tok_rows)
    source = token // tok_rows
    earlier = (token[:, None] > token[None, :]) & (source[:, None] == source[None, :])
    rank = jnp.dot(
        earlier.astype(jnp.bfloat16), member.astype(jnp.bfloat16), preferred_element_type=jnp.float32
    )
    rank = jnp.where(member, rank, -1.0)
    half_width = gate_halves.shape[2]
    if halves_dev == 1:
        parity = lax.axis_index(DEVICES) % 2
        other_gate, other_up, other_down = from_partner(
            (gate_halves, up_halves, down_halves), DEVICES, 0
        )
        first_side = parity == 0
        stack = lambda own, other: jnp.where(
            first_side, jnp.stack([own, other], 1), jnp.stack([other, own], 1)
        )
        gate_w, up_w, down_w = (
            stack(gate_halves, other_gate),
            stack(up_halves, other_up),
            stack(down_halves, other_down),
        )
        items_dev = 1
    else:
        items_dev = halves_dev // 2
        gate_w = gate_halves.reshape(items_dev, 2, feature_width, half_width)
        up_w = up_halves.reshape(items_dev, 2, feature_width, half_width)
        down_w = down_halves.reshape(items_dev, 2, half_width, feature_width)
    slot_count = experts * capacity // (devices * items_dev)
    f32 = jnp.float32
    exchange = functools.partial(
        lax.all_to_all, axis_name=PLANE, split_axis=0, concat_axis=0, tiled=True
    )
    plane = devices // z_size
    member_place = jnp.arange(plane)
    target = (member_place // y_size * z_size + z_place) * y_size + member_place % y_size
    partial_grad = jnp.zeros((z_size * tok_rows, feature_width), f32)
    to_rows = lambda a: a.reshape(plane * z_size * slot_count, z_size * tok_rows)
    same = (jnp.arange(z_size)[:, None] == source[None, :])[None, :, None, :]
    for item in range(items_dev):
        slot = (
            target[:, None] * (items_dev * slot_count)
            + item * slot_count
            + jnp.arange(slot_count)[None, :]
        ).reshape(-1)
        slot_expert = (slot // capacity).astype(jnp.int32)
        pick = (expert_ids[:, None] == slot_expert[None, :]).astype(f32)
        slot_rank = jnp.dot(
            rank.astype(jnp.bfloat16), pick.astype(jnp.bfloat16), preferred_element_type=f32
        )
        here = slot_rank == (slot % capacity).astype(f32)[None, :]
        slot_gate = jnp.dot(gate_of, pick, precision=highest)
        here = here.T.reshape(plane, 1, slot_count, -1) & same
        weight = to_rows(jnp.where(here, slot_gate.T.reshape(plane, 1, slot_count, -1), 0.0))
        take = to_rows(here).astype(jnp.bfloat16)
        send_input = jnp.dot(take, line_input, preferred_element_type=jnp.bfloat16)
        send_grad = jnp.dot(take, line_grad, preferred_element_type=jnp.bfloat16)
        recv_input = exchange(send_input)
        recv_grad = exchange(send_grad)
        terms = swiglu_back(recv_input, recv_grad, gate_w[item], up_w[item], down_w[item])
        returned = exchange(terms)
        for piece in split_bf16(weight):
            partial_grad = partial_grad + lax.dot_general(
                piece, returned, (((0,), (0,)), ((), ())), preferred_element_type=f32
            )
    shares = lax.all_to_all(
        partial_grad.astype(jnp.bfloat16), "z", split_axis=0, concat_axis=0, tiled=True
    ).reshape(z_size, tok_rows, feature_width)
    moe_grad = jnp.sum(shares.astype(f32), axis=0)
    resid_grad = (out_grad.astype(f32) + moe_grad).astype(jnp.bfloat16)
    inner_dev = out_proj.shape[0]
    heads_dev = skip_gain.shape[0]
    head_dim = inner_dev // heads_dev
    seq_rows, state_dim = b_proj.shape
    block_len = BLOCK
    block_count = seq_rows // block_len
    decay = log_decay.reshape(heads_dev, block_count, block_len)
    causal = jnp.arange(block_len)[:, None] >= jnp.arange(block_len)[None, :]
    within = jnp.einsum("hbr,tr->hbt", decay, causal.astype(f32), precision=highest)
    block_sum = within[:, :, -1]
    later_sum = [jnp.zeros((heads_dev,), f32)]
    for block in reversed(range(1, block_count)):
        later_sum.insert(0, later_sum[0] + block_sum[:, block])
    tail = jnp.stack(later_sum, 1)
    total = later_sum[0] + block_sum[:, 0]
    totals = lax.all_gather(total, "seq")
    seq_count, place = lax.axis_size("seq"), lax.axis_index("seq")
    between = jnp.zeros((heads_dev,), f32)
    carried = []
    for source in range(seq_count):
        carried.append(jnp.where(source > place, jnp.exp(between), 0.0))
        between = between + jnp.where(source > place, totals[source], 0.0)
    b_blocks = b_proj.reshape(block_count, block_len, state_dim)
    c_blocks = c_proj.reshape(block_count, block_len, state_dim)
    x_blocks = ssd_x.reshape(block_count, block_len, heads_dev, head_dim)
    scores = jnp.einsum("btn,bsn->bts", c_blocks, b_blocks, precision=highest)
    log_gap = within[:, :, :, None] - within[:, :, None, :]
    weights = jnp.where(causal, jnp.exp(jnp.where(causal, log_gap, 0.0)), 0.0) * scores[None]
    to_start = jnp.exp(within)
    to_end = jnp.exp(block_sum[:, :, None] - within)
    block_decay = jnp.exp(block_sum)
    ssd_grad = jnp.einsum(
        "td,kd->tk",
        gather([resid_grad], True, 1)[0],
        out_proj,
        preferred_element_type=jnp.float32,
    )
    g_blocks = ssd_grad.reshape(block_count, block_len, heads_dev, head_dim)
    intra_x = jnp.einsum("hbts,bthp->bshp", weights, g_blocks, precision=highest)
    inner_prod = jnp.einsum("bthp,bshp->hbts", g_blocks, x_blocks, precision=highest)
    intra_b = jnp.einsum("hbts,btn->bsn", weights * inner_prod, c_blocks, precision=highest)
    block_state = jnp.einsum("hbt,bthp,btn->bhpn", to_start, g_blocks, c_blocks, precision=highest)

    carry = jnp.zeros((heads_dev, head_dim, state_dim), f32)
    after = []
    for block in reversed(range(block_count)):
        after.insert(0, carry)
        carry = block_decay[:, block, None, None] * carry + block_state[block]
    states = lax.all_gather(carry, "seq")
    incoming = sum(carried[s][:, None, None] * states[s] for s in range(seq_count))
    future = jnp.stack(after) + jnp.exp(tail).T[:, :, None, None] * incoming[None]
    cross_x = jnp.einsum("hbs,bsn,bhpn->bshp", to_end, b_blocks, future, precision=highest)
    grad_x = intra_x + cross_x + skip_gain[None, None, :, None] * g_blocks
    cross_b = jnp.einsum("hbs,bshp,bhpn->bsn", to_end, x_blocks, future, precision=highest)
    partial_b = (intra_b + cross_b).reshape(seq_rows, state_dim)
    parts = lax.all_to_all(partial_b, HEAD, split_axis=0, concat_axis=0, tiled=True)
    b_grad = jnp.sum(parts.reshape(lax.axis_size(HEAD), -1, state_dim), axis=0)
    return (resid_grad, grad_x.reshape(seq_rows, inner_dev), b_grad)


def solution(mesh):
    seq, head = mesh.shape["seq"], mesh.shape["head"]
    levels = {getattr(d, "coords", (0, 0, 0))[2] for d in mesh.devices.flat}
    z_size = len(levels) if head % len(levels) == 0 else 1
    mesh = Mesh(mesh.devices.reshape(seq, z_size, head // z_size), DEVICES)
    return jax.shard_map(
        shards,
        mesh=mesh,
        in_specs=(
            P(DEVICES, None),
            P(DEVICES, None),
            P(DEVICES, None),
            P(DEVICES, None),
            P(DEVICES, None, None),
            P(DEVICES, None, None),
            P(DEVICES, None, None),
            P(HEAD, None),
            P("seq", HEAD),
            P("seq", None),
            P("seq", None),
            P(HEAD, "seq"),
            P(HEAD),
        ),
        out_specs=(P(DEVICES, None), P("seq", HEAD), P(DEVICES, None)),
        check_vma=False,
    )
```

```python
import functools
import jax
import jax.numpy as jnp
from jax import lax
from jax.experimental import pallas as pl
from jax.experimental.pallas import tpu as pltpu
from jax.sharding import Mesh, PartitionSpec as P

BLOCK = 256
HEAD = ("z", "y")
DEVICES = ("seq", "z", "y")
PLANE = ("seq", "y")


def from_partner(shard, axis, distance):
    return lax.ppermute(shard, axis, [(i, i ^ 1 << distance) for i in range(lax.axis_size(axis))])


def expert_kernel(x_ref, g_ref, gate_ref, up_ref, down_ref, out_ref):
    last = (((1,), (1,)), ((), ()))
    f32 = jnp.float32
    width = x_ref.shape[-1]
    x, g = x_ref[...].reshape(-1, width), g_ref[...].reshape(-1, width)
    total = None
    for j in range(gate_ref.shape[0]):
        gate_act = jnp.dot(x, gate_ref[j], preferred_element_type=f32)
        up_act = jnp.dot(x, up_ref[j], preferred_element_type=f32)
        hidden_grad = lax.dot_general(g, down_ref[j], last, preferred_element_type=f32)
        s = jax.nn.sigmoid(gate_act)
        gate_grad = (hidden_grad * up_act * s * (1.0 + gate_act * (1.0 - s))).astype(jnp.bfloat16)
        up_grad = (hidden_grad * gate_act * s).astype(jnp.bfloat16)
        term = lax.dot_general(gate_grad, gate_ref[j], last, preferred_element_type=f32)
        term = term + lax.dot_general(up_grad, up_ref[j], last, preferred_element_type=f32)
        total = term if total is None else total + term
    out_ref[...] = total.reshape(out_ref.shape).astype(out_ref.dtype)


def swiglu_back(item, rows_in, rows_grad, gate, up, down):
    groups, _, slots, width = rows_in.shape
    halves, hidden = gate.shape[1], gate.shape[3]
    rows = groups * slots
    tile = max(1, min(groups, 256 // slots))
    row = pl.BlockSpec((tile, None, slots, width), lambda i: (i, item, 0, 0))
    whole = lambda a: pl.BlockSpec((None, *a.shape[1:]), lambda i: (item, 0, 0, 0))
    return pl.pallas_call(
        expert_kernel,
        grid=(groups // tile,),
        in_specs=[row, row, whole(gate), whole(up), whole(down)],
        out_specs=pl.BlockSpec((tile, slots, width), lambda i: (i, 0, 0)),
        out_shape=jax.ShapeDtypeStruct((groups, slots, width), jnp.bfloat16),
        compiler_params=pltpu.CompilerParams(vmem_limit_bytes=48 * 1024 * 1024),
        cost_estimate=pl.CostEstimate(
            flops=10 * rows * width * halves * hidden,
            bytes_accessed=6 * rows * width + 6 * halves * width * hidden,
            transcendentals=rows * halves * hidden,
        ),
    )(rows_in, rows_grad, gate, up, down)


def dispatch_kernel(z_size, y_size, plane, x_ref, g_ref, take_ref, x_out, g_out, *scratch):
    line, packed, z_send, z_recv, p_send, p_recv, local_sem, self_sem = scratch
    own, out = (x_ref, g_ref), (x_out, g_out)
    seq, z, y = (lax.axis_index(a) for a in DEVICES)
    mesh_ids = pl.DeviceIdType.MESH
    me = seq * y_size + y
    chunk, width = x_out.shape[2:]
    local = [pltpu.make_async_copy(own[i], line.at[i, z], local_sem.at[i]) for i in range(2)]
    for copy in local:
        copy.start()

    def member(shift):
        q = lax.rem(me + shift, plane)
        return (q // y_size, z, lax.rem(q, y_size))

    barrier = pltpu.get_barrier_semaphore()
    for dz in range(1, z_size):
        pl.semaphore_signal(
            barrier, inc=1, device_id=(seq, lax.rem(z + dz, z_size), y), device_id_type=mesh_ids
        )
    for shift in range(1, plane):
        pl.semaphore_signal(barrier, inc=1, device_id=member(shift), device_id_type=mesh_ids)
    pl.semaphore_wait(barrier, z_size + plane - 2)
    for copy in local:
        copy.wait()

    def z_copy(i, way, step, block, target):
        return pltpu.make_async_remote_copy(
            src_ref=line.at[i, block],
            dst_ref=line.at[i, block],
            send_sem=z_send.at[i, way, step],
            recv_sem=z_recv.at[i, way, step],
            device_id=(seq, target, y),
            device_id_type=mesh_ids,
        )

    def plane_copy(i, block, shift, source):
        return pltpu.make_async_remote_copy(
            src_ref=packed.at[i, block, lax.rem(me + shift, plane)],
            dst_ref=out[i].at[source, block],
            send_sem=p_send.at[i, block, shift - 1],
            recv_sem=p_recv.at[i, block, shift - 1],
            device_id=member(shift),
            device_id_type=mesh_ids,
        )

    def keep(i, block):
        return pltpu.make_async_copy(
            packed.at[i, block, me], out[i].at[me, block], self_sem.at[i, block]
        )

    def process(i, block):
        rows = jnp.dot(take_ref[block], line[i, block], preferred_element_type=jnp.float32)
        packed[i, block] = rows.reshape(plane, chunk, width).astype(packed.dtype)
        keep(i, block).start()

        @pl.loop(1, plane)
        def _(shift):
            plane_copy(i, block, shift, me).start()

    def within(index):
        return jnp.logical_and(index >= 0, index < z_size)

    ways = ((0, 1), (1, -1))
    for step in range(z_size - 1):
        for i in range(2):
            for way, sign in ways:
                block = z - sign * step

                @pl.when(jnp.logical_and(within(block), within(z + sign)))
                def _():
                    if step:
                        z_copy(i, way, step - 1, block, z).wait_recv()
                    z_copy(i, way, step, block, z + sign).start()

        for way, sign in ways:
            block = z - sign * step

            if step:

                @pl.when(jnp.logical_and(within(block), jnp.logical_not(within(z + sign))))
                def _():
                    for i in range(2):
                        z_copy(i, way, step - 1, block, z).wait_recv()

            if step:

                @pl.when(within(block))
                def _():
                    for i in range(2):
                        process(i, block)

        if step == 0:
            for i in range(2):
                process(i, z)
    if z_size == 1:
        for i in range(2):
            process(i, z)
    else:
        for way, sign in ways:
            arriving = z - sign * (z_size - 1)

            @pl.when(within(arriving))
            def _():
                for i in range(2):
                    z_copy(i, way, z_size - 2, arriving, z).wait_recv()
                    process(i, arriving)

    for i in range(2):
        for block in range(z_size):
            keep(i, block).wait()

            @pl.loop(1, plane)
            def _(shift):
                copy = plane_copy(i, block, shift, lax.rem(me + plane - shift, plane))
                copy.wait_send()
                copy.wait_recv()

    for step in range(z_size - 1):
        for way, sign in ways:
            block = z - sign * step

            @pl.when(jnp.logical_and(within(block), within(z + sign)))
            def _():
                for i in range(2):
                    z_copy(i, way, step, block, z + sign).wait_send()


def dispatch(rows_in, rows_grad, take, plane, collective_id):
    z_size, y_size = lax.axis_size("z"), lax.axis_size("y")
    rows, width = rows_in.shape
    chunk = take.shape[1] // plane
    vmem = pl.BlockSpec(memory_space=pltpu.VMEM)
    dma = pltpu.SemaphoreType.DMA
    steps = max(1, z_size - 1)
    return pl.pallas_call(
        functools.partial(dispatch_kernel, z_size, y_size, plane),
        in_specs=[vmem] * 3,
        out_specs=[vmem] * 2,
        out_shape=[jax.ShapeDtypeStruct((plane, z_size, chunk, width), jnp.bfloat16)] * 2,
        scratch_shapes=[
            pltpu.VMEM((2, z_size, rows, width), jnp.bfloat16),
            pltpu.VMEM((2, z_size, plane, chunk, width), jnp.bfloat16),
            dma((2, 2, steps)),
            dma((2, 2, steps)),
            dma((2, z_size, plane - 1)),
            dma((2, z_size, plane - 1)),
            dma((2,)),
            dma((2, z_size)),
        ],
        compiler_params=pltpu.CompilerParams(
            collective_id=collective_id,
            has_side_effects=True,
            vmem_limit_bytes=48 * 1024 * 1024,
        ),
    )(rows_in, rows_grad, take)


def gather_kernel(count, z_size, y_size, *refs):
    own, out = refs[:count], refs[count : 2 * count]
    z_send, z_recv, y_send, y_recv, local_sem = refs[2 * count :]
    seq, z, y = (lax.axis_index(a) for a in DEVICES)
    mesh_ids = pl.DeviceIdType.MESH
    place = lambda block, column: block * y_size + column if y_size > 1 else block

    local = [
        pltpu.make_async_copy(own[i], out[i].at[place(z, y)], local_sem.at[i]) for i in range(count)
    ]
    for copy in local:
        copy.start()
    barrier = pltpu.get_barrier_semaphore()
    signals = 0
    for dz in range(z_size):
        for dy in range(y_size):
            if dz or dy:
                peer = (seq, lax.rem(z + dz, z_size), lax.rem(y + dy, y_size) if y_size > 1 else y)
                pl.semaphore_signal(barrier, inc=1, device_id=peer, device_id_type=mesh_ids)
                signals += 1
    pl.semaphore_wait(barrier, signals)
    for copy in local:
        copy.wait()

    def z_copy(i, way, step, block, target):
        ref = out[i].at[place(block, y)]
        return pltpu.make_async_remote_copy(
            src_ref=ref,
            dst_ref=ref,
            send_sem=z_send.at[i, way, step],
            recv_sem=z_recv.at[i, way, step],
            device_id=(seq, target, y),
            device_id_type=mesh_ids,
        )

    def y_copy(i, shift, way, step, block, column):
        ref = out[i].at[place(block, column)]
        return pltpu.make_async_remote_copy(
            src_ref=ref,
            dst_ref=ref,
            send_sem=y_send.at[i, shift - 1, way, step],
            recv_sem=y_recv.at[i, shift - 1, way, step],
            device_id=(seq, z, lax.rem(y + shift, y_size)),
            device_id_type=mesh_ids,
        )

    def within(index):
        return jnp.logical_and(index >= 0, index < z_size)

    ways = ((0, 1), (1, -1))

    def across(run, way, step, block, sending):
        for i in range(count):
            for shift in range(1, y_size):
                column = y if sending else lax.rem(y + y_size - shift, y_size)
                run(y_copy(i, shift, way, step, block, column))

    start = lambda c: c.start()
    wait_send = lambda c: c.wait_send()
    wait_recv = lambda c: c.wait_recv()
    for step in range(z_size - 1):
        for way, sign in ways:
            block = z - sign * step

            @pl.when(jnp.logical_and(within(block), within(z + sign)))
            def _():
                for i in range(count):
                    z_copy(i, way, step, block, z + sign).start()

        if step == 0:
            across(start, 0, 0, z, True)
        for way, sign in ways:
            arriving = z - sign * (step + 1)

            @pl.when(within(arriving))
            def _():
                for i in range(count):
                    z_copy(i, way, step, arriving, z).wait_recv()
                across(start, way, step + 1, arriving, True)

    if z_size == 1:
        across(start, 0, 0, z, True)
    across(wait_send, 0, 0, z, True)
    across(wait_recv, 0, 0, z, False)
    for step in range(z_size - 1):
        for way, sign in ways:
            block = z - sign * step
            arriving = z - sign * (step + 1)

            @pl.when(jnp.logical_and(within(block), within(z + sign)))
            def _():
                for i in range(count):
                    z_copy(i, way, step, block, z + sign).wait_send()

            @pl.when(within(arriving))
            def _():
                across(wait_send, way, step + 1, arriving, True)
                across(wait_recv, way, step + 1, arriving, False)


def gather(arrays, with_y, collective_id):
    z_size = lax.axis_size("z")
    y_size = lax.axis_size("y") if with_y else 1
    count = len(arrays)
    vmem = pl.BlockSpec(memory_space=pltpu.VMEM)
    dma = pltpu.SemaphoreType.DMA
    steps = max(1, z_size - 1)
    out = pl.pallas_call(
        functools.partial(gather_kernel, count, z_size, y_size),
        in_specs=[vmem] * count,
        out_specs=[vmem] * count,
        out_shape=[jax.ShapeDtypeStruct((z_size * y_size, *a.shape), a.dtype) for a in arrays],
        scratch_shapes=[
            dma((count, 2, steps)),
            dma((count, 2, steps)),
            dma((count, max(1, y_size - 1), 2, z_size)),
            dma((count, max(1, y_size - 1), 2, z_size)),
            dma((count,)),
        ],
        compiler_params=pltpu.CompilerParams(
            collective_id=collective_id,
            has_side_effects=True,
            vmem_limit_bytes=32 * 1024 * 1024,
        ),
    )(*arrays)
    return [a.reshape(-1, a.shape[-1]) for a in out]


def split_bf16(a):
    high = lax.reduce_precision(a, 8, 7).astype(jnp.bfloat16)
    return high, (a - high.astype(jnp.float32)).astype(jnp.bfloat16)


def shards(
    moe_input,
    out_grad,
    route_ids,
    route_gates,
    gate_halves,
    up_halves,
    down_halves,
    out_proj,
    ssd_x,
    b_proj,
    c_proj,
    log_decay,
    skip_gain,
):
    highest = lax.Precision.HIGHEST
    tok_rows, feature_width = moe_input.shape
    top_count = route_ids.shape[1]
    devices = lax.axis_size(DEVICES)
    halves_dev = gate_halves.shape[0]
    experts = devices * halves_dev // 2
    capacity = tok_rows // 8
    expert_ids = jnp.arange(experts, dtype=jnp.int32)
    z_size, y_size, z_place = lax.axis_size("z"), lax.axis_size("y"), lax.axis_index("z")
    meta = jnp.concatenate([route_ids.astype(jnp.float32), route_gates], axis=1)
    meta = jnp.pad(meta, ((0, 0), (0, -meta.shape[1] % 128)))
    (line_meta,) = gather([meta], False, 0)
    line_ids = line_meta[:, :top_count].astype(jnp.int32)
    line_gates = line_meta[:, top_count : 2 * top_count]
    chosen = line_ids[:, :, None] == expert_ids[None, None, :]
    member = jnp.any(chosen, axis=1)
    gate_of = jnp.sum(jnp.where(chosen, line_gates[:, :, None], 0.0), axis=1)
    token = jnp.arange(z_size * tok_rows)
    source = token // tok_rows
    earlier = (token[:, None] > token[None, :]) & (source[:, None] == source[None, :])
    rank = jnp.dot(
        earlier.astype(jnp.bfloat16), member.astype(jnp.bfloat16), preferred_element_type=jnp.float32
    )
    rank = jnp.where(member, rank, -1.0)
    half_width = gate_halves.shape[2]
    if halves_dev == 1:
        parity = lax.axis_index(DEVICES) % 2
        other_gate, other_up, other_down = from_partner(
            (gate_halves, up_halves, down_halves), DEVICES, 0
        )
        first_side = parity == 0
        stack = lambda own, other: jnp.where(
            first_side, jnp.stack([own, other], 1), jnp.stack([other, own], 1)
        )
        gate_w, up_w, down_w = (
            stack(gate_halves, other_gate),
            stack(up_halves, other_up),
            stack(down_halves, other_down),
        )
        items_dev = 1
    else:
        items_dev = halves_dev // 2
        gate_w = gate_halves.reshape(items_dev, 2, feature_width, half_width)
        up_w = up_halves.reshape(items_dev, 2, feature_width, half_width)
        down_w = down_halves.reshape(items_dev, 2, half_width, feature_width)
    slot_count = experts * capacity // (devices * items_dev)
    f32 = jnp.float32
    exchange = functools.partial(
        lax.all_to_all, axis_name=PLANE, split_axis=0, concat_axis=0, tiled=True
    )
    plane = devices // z_size
    member_place = jnp.arange(plane)
    target = (member_place // y_size * z_size + z_place) * y_size + member_place % y_size
    partial_grad = jnp.zeros((z_size * tok_rows, feature_width), f32)
    to_rows = lambda a: a.reshape(plane * z_size * slot_count, z_size * tok_rows)
    same = (jnp.arange(z_size)[:, None] == source[None, :])[None, :, None, :]
    chunk = items_dev * slot_count
    slot = (target[:, None] * chunk + jnp.arange(chunk)[None, :]).reshape(-1)
    slot_expert = (slot // capacity).astype(jnp.int32)
    pick = (expert_ids[:, None] == slot_expert[None, :]).astype(f32)
    slot_rank = jnp.dot(
        rank.astype(jnp.bfloat16), pick.astype(jnp.bfloat16), preferred_element_type=f32
    )
    filled = slot_rank == (slot % capacity).astype(f32)[None, :]
    gate_all = jnp.dot(gate_of, pick, precision=highest)
    take = filled.astype(jnp.bfloat16).reshape(z_size, tok_rows, plane * chunk).transpose(0, 2, 1)
    recv_input, recv_grad = (
        a.reshape(plane * z_size, items_dev, slot_count, feature_width)
        for a in dispatch(moe_input, out_grad, take, plane, 2)
    )
    item_of = lambda a, item: a.T.reshape(plane, items_dev, slot_count, -1)[:, item, None]
    for item in range(items_dev):
        here = item_of(filled, item) & same
        weight = to_rows(jnp.where(here, item_of(gate_all, item), 0.0))
        terms = swiglu_back(item, recv_input, recv_grad, gate_w, up_w, down_w)
        terms = terms.reshape(-1, feature_width)
        returned = exchange(terms)
        for piece in split_bf16(weight):
            partial_grad = partial_grad + lax.dot_general(
                piece, returned, (((0,), (0,)), ((), ())), preferred_element_type=f32
            )
    shares = lax.all_to_all(
        partial_grad.astype(jnp.bfloat16), "z", split_axis=0, concat_axis=0, tiled=True
    ).reshape(z_size, tok_rows, feature_width)
    moe_grad = jnp.sum(shares.astype(f32), axis=0)
    resid_grad = (out_grad.astype(f32) + moe_grad).astype(jnp.bfloat16)
    inner_dev = out_proj.shape[0]
    heads_dev = skip_gain.shape[0]
    head_dim = inner_dev // heads_dev
    seq_rows, state_dim = b_proj.shape
    block_len = BLOCK
    block_count = seq_rows // block_len
    decay = log_decay.reshape(heads_dev, block_count, block_len)
    causal = jnp.arange(block_len)[:, None] >= jnp.arange(block_len)[None, :]
    within = jnp.einsum("hbr,tr->hbt", decay, causal.astype(f32), precision=highest)
    block_sum = within[:, :, -1]
    later_sum = [jnp.zeros((heads_dev,), f32)]
    for block in reversed(range(1, block_count)):
        later_sum.insert(0, later_sum[0] + block_sum[:, block])
    tail = jnp.stack(later_sum, 1)
    total = later_sum[0] + block_sum[:, 0]
    totals = lax.all_gather(total, "seq")
    seq_count, place = lax.axis_size("seq"), lax.axis_index("seq")
    between = jnp.zeros((heads_dev,), f32)
    carried = []
    for source in range(seq_count):
        carried.append(jnp.where(source > place, jnp.exp(between), 0.0))
        between = between + jnp.where(source > place, totals[source], 0.0)
    b_blocks = b_proj.reshape(block_count, block_len, state_dim)
    c_blocks = c_proj.reshape(block_count, block_len, state_dim)
    x_blocks = ssd_x.reshape(block_count, block_len, heads_dev, head_dim)
    scores = jnp.einsum("btn,bsn->bts", c_blocks, b_blocks, precision=highest)
    log_gap = within[:, :, :, None] - within[:, :, None, :]
    weights = jnp.where(causal, jnp.exp(jnp.where(causal, log_gap, 0.0)), 0.0) * scores[None]
    to_start = jnp.exp(within)
    to_end = jnp.exp(block_sum[:, :, None] - within)
    block_decay = jnp.exp(block_sum)
    ssd_grad = jnp.einsum(
        "td,kd->tk",
        gather([resid_grad], True, 1)[0],
        out_proj,
        preferred_element_type=jnp.float32,
    )
    g_blocks = ssd_grad.reshape(block_count, block_len, heads_dev, head_dim)
    intra_x = jnp.einsum("hbts,bthp->bshp", weights, g_blocks, precision=highest)
    inner_prod = jnp.einsum("bthp,bshp->hbts", g_blocks, x_blocks, precision=highest)
    intra_b = jnp.einsum("hbts,btn->bsn", weights * inner_prod, c_blocks, precision=highest)
    block_state = jnp.einsum("hbt,bthp,btn->bhpn", to_start, g_blocks, c_blocks, precision=highest)

    carry = jnp.zeros((heads_dev, head_dim, state_dim), f32)
    after = []
    for block in reversed(range(block_count)):
        after.insert(0, carry)
        carry = block_decay[:, block, None, None] * carry + block_state[block]
    states = lax.all_gather(carry, "seq")
    incoming = sum(carried[s][:, None, None] * states[s] for s in range(seq_count))
    future = jnp.stack(after) + jnp.exp(tail).T[:, :, None, None] * incoming[None]
    cross_x = jnp.einsum("hbs,bsn,bhpn->bshp", to_end, b_blocks, future, precision=highest)
    grad_x = intra_x + cross_x + skip_gain[None, None, :, None] * g_blocks
    cross_b = jnp.einsum("hbs,bshp,bhpn->bsn", to_end, x_blocks, future, precision=highest)
    partial_b = (intra_b + cross_b).reshape(seq_rows, state_dim)
    parts = lax.all_to_all(partial_b, HEAD, split_axis=0, concat_axis=0, tiled=True)
    b_grad = jnp.sum(parts.reshape(lax.axis_size(HEAD), -1, state_dim), axis=0)
    return (resid_grad, grad_x.reshape(seq_rows, inner_dev), b_grad)


def solution(mesh):
    seq, head = mesh.shape["seq"], mesh.shape["head"]
    levels = {getattr(d, "coords", (0, 0, 0))[2] for d in mesh.devices.flat}
    z_size = len(levels) if head % len(levels) == 0 else 1
    mesh = Mesh(mesh.devices.reshape(seq, z_size, head // z_size), DEVICES)
    return jax.shard_map(
        shards,
        mesh=mesh,
        in_specs=(
            P(DEVICES, None),
            P(DEVICES, None),
            P(DEVICES, None),
            P(DEVICES, None),
            P(DEVICES, None, None),
            P(DEVICES, None, None),
            P(DEVICES, None, None),
            P(HEAD, None),
            P("seq", HEAD),
            P("seq", None),
            P("seq", None),
            P(HEAD, "seq"),
            P(HEAD),
        ),
        out_specs=(P(DEVICES, None), P("seq", HEAD), P(DEVICES, None)),
        check_vma=False,
    )
```

```python
import functools
import jax
import jax.numpy as jnp
from jax import lax
from jax.experimental import pallas as pl
from jax.experimental.pallas import tpu as pltpu
from jax.sharding import Mesh, PartitionSpec as P

BLOCK = 256
HEAD = ("z", "y")
DEVICES = ("seq", "z", "y")
PLANE = ("seq", "y")


def from_partner(shard, axis, distance):
    return lax.ppermute(shard, axis, [(i, i ^ 1 << distance) for i in range(lax.axis_size(axis))])


def expert_kernel(x_ref, g_ref, gate_ref, up_ref, down_ref, out_ref):
    last = (((1,), (1,)), ((), ()))
    f32 = jnp.float32
    width = x_ref.shape[-1]
    x, g = x_ref[...].reshape(-1, width), g_ref[...].reshape(-1, width)
    total = None
    for j in range(gate_ref.shape[0]):
        gate_act = jnp.dot(x, gate_ref[j], preferred_element_type=f32)
        up_act = jnp.dot(x, up_ref[j], preferred_element_type=f32)
        hidden_grad = lax.dot_general(g, down_ref[j], last, preferred_element_type=f32)
        s = jax.nn.sigmoid(gate_act)
        gate_grad = (hidden_grad * up_act * s * (1.0 + gate_act * (1.0 - s))).astype(jnp.bfloat16)
        up_grad = (hidden_grad * gate_act * s).astype(jnp.bfloat16)
        term = lax.dot_general(gate_grad, gate_ref[j], last, preferred_element_type=f32)
        term = term + lax.dot_general(up_grad, up_ref[j], last, preferred_element_type=f32)
        total = term if total is None else total + term
    out_ref[...] = total.reshape(out_ref.shape).astype(out_ref.dtype)


def swiglu_back(item, rows_in, rows_grad, gate, up, down):
    groups, _, slots, width = rows_in.shape
    halves, hidden = gate.shape[1], gate.shape[3]
    rows = groups * slots
    tile = max(1, min(groups, 256 // slots))
    row = pl.BlockSpec((tile, None, slots, width), lambda i: (i, item, 0, 0))
    whole = lambda a: pl.BlockSpec((None, *a.shape[1:]), lambda i: (item, 0, 0, 0))
    return pl.pallas_call(
        expert_kernel,
        grid=(groups // tile,),
        in_specs=[row, row, whole(gate), whole(up), whole(down)],
        out_specs=pl.BlockSpec((tile, slots, width), lambda i: (i, 0, 0)),
        out_shape=jax.ShapeDtypeStruct((groups, slots, width), jnp.bfloat16),
        compiler_params=pltpu.CompilerParams(vmem_limit_bytes=48 * 1024 * 1024),
        cost_estimate=pl.CostEstimate(
            flops=10 * rows * width * halves * hidden,
            bytes_accessed=6 * rows * width + 6 * halves * width * hidden,
            transcendentals=rows * halves * hidden,
        ),
    )(rows_in, rows_grad, gate, up, down)


def dispatch_kernel(z_size, y_size, plane, x_ref, g_ref, take_ref, x_out, g_out, *scratch):
    line, packed, z_send, z_recv, p_send, p_recv, local_sem, self_sem = scratch
    own, out = (x_ref, g_ref), (x_out, g_out)
    seq, z, y = (lax.axis_index(a) for a in DEVICES)
    mesh_ids = pl.DeviceIdType.MESH
    me = seq * y_size + y
    chunk, width = x_out.shape[2:]
    local = [pltpu.make_async_copy(own[i], line.at[i, z], local_sem.at[i]) for i in range(2)]
    for copy in local:
        copy.start()

    def member(shift):
        q = lax.rem(me + shift, plane)
        return (q // y_size, z, lax.rem(q, y_size))

    barrier = pltpu.get_barrier_semaphore()
    for dz in range(1, z_size):
        pl.semaphore_signal(
            barrier, inc=1, device_id=(seq, lax.rem(z + dz, z_size), y), device_id_type=mesh_ids
        )
    for shift in range(1, plane):
        pl.semaphore_signal(barrier, inc=1, device_id=member(shift), device_id_type=mesh_ids)
    pl.semaphore_wait(barrier, z_size + plane - 2)
    for copy in local:
        copy.wait()

    def z_copy(i, way, step, block, target):
        return pltpu.make_async_remote_copy(
            src_ref=line.at[i, block],
            dst_ref=line.at[i, block],
            send_sem=z_send.at[i, way, step],
            recv_sem=z_recv.at[i, way, step],
            device_id=(seq, target, y),
            device_id_type=mesh_ids,
        )

    def plane_copy(i, block, shift, source):
        return pltpu.make_async_remote_copy(
            src_ref=packed.at[i, block, lax.rem(me + shift, plane)],
            dst_ref=out[i].at[source, block],
            send_sem=p_send.at[i, block, shift - 1],
            recv_sem=p_recv.at[i, block, shift - 1],
            device_id=member(shift),
            device_id_type=mesh_ids,
        )

    def keep(i, block):
        return pltpu.make_async_copy(
            packed.at[i, block, me], out[i].at[me, block], self_sem.at[i, block]
        )

    def process(i, block):
        rows = jnp.dot(take_ref[block], line[i, block], preferred_element_type=jnp.float32)
        packed[i, block] = rows.reshape(plane, chunk, width).astype(packed.dtype)
        keep(i, block).start()

        @pl.loop(1, plane)
        def _(shift):
            plane_copy(i, block, shift, me).start()

    def within(index):
        return jnp.logical_and(index >= 0, index < z_size)

    ways = ((0, 1), (1, -1))
    for step in range(z_size - 1):
        for i in range(2):
            for way, sign in ways:
                block = z - sign * step

                @pl.when(jnp.logical_and(within(block), within(z + sign)))
                def _():
                    if step:
                        z_copy(i, way, step - 1, block, z).wait_recv()
                    z_copy(i, way, step, block, z + sign).start()

        for way, sign in ways:
            block = z - sign * step

            if step:

                @pl.when(jnp.logical_and(within(block), jnp.logical_not(within(z + sign))))
                def _():
                    for i in range(2):
                        z_copy(i, way, step - 1, block, z).wait_recv()

            if step:

                @pl.when(within(block))
                def _():
                    for i in range(2):
                        process(i, block)

        if step == 0:
            for i in range(2):
                process(i, z)
    if z_size == 1:
        for i in range(2):
            process(i, z)
    else:
        for way, sign in ways:
            arriving = z - sign * (z_size - 1)

            @pl.when(within(arriving))
            def _():
                for i in range(2):
                    z_copy(i, way, z_size - 2, arriving, z).wait_recv()
                    process(i, arriving)

    for i in range(2):
        for block in range(z_size):
            keep(i, block).wait()

            @pl.loop(1, plane)
            def _(shift):
                copy = plane_copy(i, block, shift, lax.rem(me + plane - shift, plane))
                copy.wait_send()
                copy.wait_recv()

    for step in range(z_size - 1):
        for way, sign in ways:
            block = z - sign * step

            @pl.when(jnp.logical_and(within(block), within(z + sign)))
            def _():
                for i in range(2):
                    z_copy(i, way, step, block, z + sign).wait_send()


def dispatch(rows_in, rows_grad, take, plane, collective_id):
    z_size, y_size = lax.axis_size("z"), lax.axis_size("y")
    rows, width = rows_in.shape
    chunk = take.shape[1] // plane
    vmem = pl.BlockSpec(memory_space=pltpu.VMEM)
    dma = pltpu.SemaphoreType.DMA
    steps = max(1, z_size - 1)
    return pl.pallas_call(
        functools.partial(dispatch_kernel, z_size, y_size, plane),
        in_specs=[vmem] * 3,
        out_specs=[vmem] * 2,
        out_shape=[jax.ShapeDtypeStruct((plane, z_size, chunk, width), jnp.bfloat16)] * 2,
        scratch_shapes=[
            pltpu.VMEM((2, z_size, rows, width), jnp.bfloat16),
            pltpu.VMEM((2, z_size, plane, chunk, width), jnp.bfloat16),
            dma((2, 2, steps)),
            dma((2, 2, steps)),
            dma((2, z_size, plane - 1)),
            dma((2, z_size, plane - 1)),
            dma((2,)),
            dma((2, z_size)),
        ],
        compiler_params=pltpu.CompilerParams(
            collective_id=collective_id,
            has_side_effects=True,
            vmem_limit_bytes=48 * 1024 * 1024,
        ),
    )(rows_in, rows_grad, take)


def gather_kernel(count, z_size, y_size, *refs):
    own, out = refs[:count], refs[count : 2 * count]
    z_send, z_recv, y_send, y_recv, local_sem = refs[2 * count :]
    seq, z, y = (lax.axis_index(a) for a in DEVICES)
    mesh_ids = pl.DeviceIdType.MESH
    place = lambda block, column: block * y_size + column if y_size > 1 else block

    local = [
        pltpu.make_async_copy(own[i], out[i].at[place(z, y)], local_sem.at[i]) for i in range(count)
    ]
    for copy in local:
        copy.start()
    barrier = pltpu.get_barrier_semaphore()
    signals = 0
    for dz in range(z_size):
        for dy in range(y_size):
            if dz or dy:
                peer = (seq, lax.rem(z + dz, z_size), lax.rem(y + dy, y_size) if y_size > 1 else y)
                pl.semaphore_signal(barrier, inc=1, device_id=peer, device_id_type=mesh_ids)
                signals += 1
    pl.semaphore_wait(barrier, signals)
    for copy in local:
        copy.wait()

    def z_copy(i, way, step, block, target):
        ref = out[i].at[place(block, y)]
        return pltpu.make_async_remote_copy(
            src_ref=ref,
            dst_ref=ref,
            send_sem=z_send.at[i, way, step],
            recv_sem=z_recv.at[i, way, step],
            device_id=(seq, target, y),
            device_id_type=mesh_ids,
        )

    def y_copy(i, shift, way, step, block, column):
        ref = out[i].at[place(block, column)]
        return pltpu.make_async_remote_copy(
            src_ref=ref,
            dst_ref=ref,
            send_sem=y_send.at[i, shift - 1, way, step],
            recv_sem=y_recv.at[i, shift - 1, way, step],
            device_id=(seq, z, lax.rem(y + shift, y_size)),
            device_id_type=mesh_ids,
        )

    def within(index):
        return jnp.logical_and(index >= 0, index < z_size)

    ways = ((0, 1), (1, -1))

    def across(run, way, step, block, sending):
        for i in range(count):
            for shift in range(1, y_size):
                column = y if sending else lax.rem(y + y_size - shift, y_size)
                run(y_copy(i, shift, way, step, block, column))

    start = lambda c: c.start()
    wait_send = lambda c: c.wait_send()
    wait_recv = lambda c: c.wait_recv()
    for step in range(z_size - 1):
        for way, sign in ways:
            block = z - sign * step

            @pl.when(jnp.logical_and(within(block), within(z + sign)))
            def _():
                for i in range(count):
                    z_copy(i, way, step, block, z + sign).start()

        if step == 0:
            across(start, 0, 0, z, True)
        for way, sign in ways:
            arriving = z - sign * (step + 1)

            @pl.when(within(arriving))
            def _():
                for i in range(count):
                    z_copy(i, way, step, arriving, z).wait_recv()
                across(start, way, step + 1, arriving, True)

    if z_size == 1:
        across(start, 0, 0, z, True)
    across(wait_send, 0, 0, z, True)
    across(wait_recv, 0, 0, z, False)
    for step in range(z_size - 1):
        for way, sign in ways:
            block = z - sign * step
            arriving = z - sign * (step + 1)

            @pl.when(jnp.logical_and(within(block), within(z + sign)))
            def _():
                for i in range(count):
                    z_copy(i, way, step, block, z + sign).wait_send()

            @pl.when(within(arriving))
            def _():
                across(wait_send, way, step + 1, arriving, True)
                across(wait_recv, way, step + 1, arriving, False)


def gather(arrays, with_y, collective_id):
    z_size = lax.axis_size("z")
    y_size = lax.axis_size("y") if with_y else 1
    count = len(arrays)
    vmem = pl.BlockSpec(memory_space=pltpu.VMEM)
    dma = pltpu.SemaphoreType.DMA
    steps = max(1, z_size - 1)
    out = pl.pallas_call(
        functools.partial(gather_kernel, count, z_size, y_size),
        in_specs=[vmem] * count,
        out_specs=[vmem] * count,
        out_shape=[jax.ShapeDtypeStruct((z_size * y_size, *a.shape), a.dtype) for a in arrays],
        scratch_shapes=[
            dma((count, 2, steps)),
            dma((count, 2, steps)),
            dma((count, max(1, y_size - 1), 2, z_size)),
            dma((count, max(1, y_size - 1), 2, z_size)),
            dma((count,)),
        ],
        compiler_params=pltpu.CompilerParams(
            collective_id=collective_id,
            has_side_effects=True,
            vmem_limit_bytes=32 * 1024 * 1024,
        ),
    )(*arrays)
    return [a.reshape(-1, a.shape[-1]) for a in out]


def split_bf16(a):
    high = lax.reduce_precision(a, 8, 7).astype(jnp.bfloat16)
    return high, (a - high.astype(jnp.float32)).astype(jnp.bfloat16)


def shards(
    moe_input,
    out_grad,
    route_ids,
    route_gates,
    gate_halves,
    up_halves,
    down_halves,
    out_proj,
    ssd_x,
    b_proj,
    c_proj,
    log_decay,
    skip_gain,
):
    highest = lax.Precision.HIGHEST
    tok_rows, feature_width = moe_input.shape
    top_count = route_ids.shape[1]
    devices = lax.axis_size(DEVICES)
    halves_dev = gate_halves.shape[0]
    experts = devices * halves_dev // 2
    capacity = tok_rows // 8
    expert_ids = jnp.arange(experts, dtype=jnp.int32)
    z_size, y_size, z_place = lax.axis_size("z"), lax.axis_size("y"), lax.axis_index("z")
    meta = jnp.concatenate([route_ids.astype(jnp.float32), route_gates], axis=1)
    meta = jnp.pad(meta, ((0, 0), (0, -meta.shape[1] % 128)))
    (line_meta,) = gather([meta], False, 0)
    line_ids = line_meta[:, :top_count].astype(jnp.int32)
    line_gates = line_meta[:, top_count : 2 * top_count]
    chosen = line_ids[:, :, None] == expert_ids[None, None, :]
    member = jnp.any(chosen, axis=1)
    gate_of = jnp.sum(jnp.where(chosen, line_gates[:, :, None], 0.0), axis=1)
    token = jnp.arange(z_size * tok_rows)
    source = token // tok_rows
    earlier = (token[:, None] > token[None, :]) & (source[:, None] == source[None, :])
    rank = jnp.dot(
        earlier.astype(jnp.bfloat16), member.astype(jnp.bfloat16), preferred_element_type=jnp.float32
    )
    rank = jnp.where(member, rank, -1.0)
    half_width = gate_halves.shape[2]
    if halves_dev == 1:
        parity = lax.axis_index(DEVICES) % 2
        other_gate, other_up, other_down = from_partner(
            (gate_halves, up_halves, down_halves), DEVICES, 0
        )
        first_side = parity == 0
        stack = lambda own, other: jnp.where(
            first_side, jnp.stack([own, other], 1), jnp.stack([other, own], 1)
        )
        gate_w, up_w, down_w = (
            stack(gate_halves, other_gate),
            stack(up_halves, other_up),
            stack(down_halves, other_down),
        )
        items_dev = 1
    else:
        items_dev = halves_dev // 2
        gate_w = gate_halves.reshape(items_dev, 2, feature_width, half_width)
        up_w = up_halves.reshape(items_dev, 2, feature_width, half_width)
        down_w = down_halves.reshape(items_dev, 2, half_width, feature_width)
    slot_count = experts * capacity // (devices * items_dev)
    f32 = jnp.float32
    exchange = functools.partial(
        lax.all_to_all, axis_name=PLANE, split_axis=0, concat_axis=0, tiled=True
    )
    plane = devices // z_size
    member_place = jnp.arange(plane)
    target = (member_place // y_size * z_size + z_place) * y_size + member_place % y_size
    partial_grad = jnp.zeros((z_size * tok_rows, feature_width), f32)
    to_rows = lambda a: a.reshape(plane * z_size * slot_count, z_size * tok_rows)
    same = (jnp.arange(z_size)[:, None] == source[None, :])[None, :, None, :]
    chunk = items_dev * slot_count
    slot = (target[:, None] * chunk + jnp.arange(chunk)[None, :]).reshape(-1)
    slot_expert = (slot // capacity).astype(jnp.int32)
    pick = (expert_ids[:, None] == slot_expert[None, :]).astype(f32)
    slot_rank = jnp.dot(
        rank.astype(jnp.bfloat16), pick.astype(jnp.bfloat16), preferred_element_type=f32
    )
    filled = slot_rank == (slot % capacity).astype(f32)[None, :]
    gate_all = jnp.dot(gate_of, pick, precision=highest)
    take = filled.astype(jnp.bfloat16).reshape(z_size, tok_rows, plane * chunk).transpose(0, 2, 1)
    recv_input, recv_grad = (
        a.reshape(plane * z_size, items_dev, slot_count, feature_width)
        for a in dispatch(moe_input, out_grad, take, plane, 2)
    )
    item_of = lambda a, item: a.T.reshape(plane, items_dev, slot_count, -1)[:, item, None]
    for item in range(items_dev):
        here = item_of(filled, item) & same
        weight = to_rows(jnp.where(here, item_of(gate_all, item), 0.0))
        terms = swiglu_back(item, recv_input, recv_grad, gate_w, up_w, down_w)
        terms = terms.reshape(-1, feature_width)
        returned = exchange(terms)
        for piece in split_bf16(weight):
            partial_grad = partial_grad + lax.dot_general(
                piece, returned, (((0,), (0,)), ((), ())), preferred_element_type=f32
            )
    shares = lax.all_to_all(
        partial_grad.astype(jnp.bfloat16), "z", split_axis=0, concat_axis=0, tiled=True
    ).reshape(z_size, tok_rows, feature_width)
    moe_grad = jnp.sum(shares.astype(f32), axis=0)
    resid_grad = (out_grad.astype(f32) + moe_grad).astype(jnp.bfloat16)
    inner_dev = out_proj.shape[0]
    heads_dev = skip_gain.shape[0]
    head_dim = inner_dev // heads_dev
    seq_rows, state_dim = b_proj.shape
    block_len = BLOCK
    block_count = seq_rows // block_len
    decay = log_decay.reshape(heads_dev, block_count, block_len)
    causal = jnp.arange(block_len)[:, None] >= jnp.arange(block_len)[None, :]
    within = jnp.einsum("hbr,tr->hbt", decay, causal.astype(f32), precision=highest)
    block_sum = within[:, :, -1]
    later_sum = [jnp.zeros((heads_dev,), f32)]
    for block in reversed(range(1, block_count)):
        later_sum.insert(0, later_sum[0] + block_sum[:, block])
    tail = jnp.stack(later_sum, 1)
    total = later_sum[0] + block_sum[:, 0]
    totals = lax.all_gather(total, "seq")
    seq_count, place = lax.axis_size("seq"), lax.axis_index("seq")
    between = jnp.zeros((heads_dev,), f32)
    carried = []
    for source in range(seq_count):
        carried.append(jnp.where(source > place, jnp.exp(between), 0.0))
        between = between + jnp.where(source > place, totals[source], 0.0)
    b_blocks = b_proj.reshape(block_count, block_len, state_dim)
    c_blocks = c_proj.reshape(block_count, block_len, state_dim)
    x_blocks = ssd_x.reshape(block_count, block_len, heads_dev, head_dim)
    scores = jnp.einsum("btn,bsn->bts", c_blocks, b_blocks, precision=highest)
    log_gap = within[:, :, :, None] - within[:, :, None, :]
    weights = jnp.where(causal, jnp.exp(jnp.where(causal, log_gap, 0.0)), 0.0) * scores[None]
    to_start = jnp.exp(within)
    to_end = jnp.exp(block_sum[:, :, None] - within)
    block_decay = jnp.exp(block_sum)
    ssd_grad = jnp.einsum(
        "td,kd->tk",
        gather([resid_grad], True, 1)[0],
        out_proj,
        preferred_element_type=jnp.float32,
    )
    g_blocks = ssd_grad.reshape(block_count, block_len, heads_dev, head_dim)
    intra_x = jnp.einsum("hbts,bthp->bshp", weights, g_blocks, precision=highest)
    inner_prod = jnp.einsum("bthp,bshp->hbts", g_blocks, x_blocks, precision=highest)
    intra_b = jnp.einsum("hbts,btn->bsn", weights * inner_prod, c_blocks, precision=highest)
    block_state = jnp.einsum("hbt,bthp,btn->bhpn", to_start, g_blocks, c_blocks, precision=highest)

    carry = jnp.zeros((heads_dev, head_dim, state_dim), f32)
    after = []
    for block in reversed(range(block_count)):
        after.insert(0, carry)
        carry = block_decay[:, block, None, None] * carry + block_state[block]
    factors = jnp.stack(carried)
    incoming = jnp.zeros_like(carry)
    for shift in range(1, seq_count):
        later = lax.ppermute(carry, "seq", [(i, i - shift) for i in range(shift, seq_count)])
        factor = factors[jnp.minimum(place + shift, seq_count - 1)]
        incoming = incoming + factor[:, None, None] * later
    future = jnp.stack(after) + jnp.exp(tail).T[:, :, None, None] * incoming[None]
    cross_x = jnp.einsum("hbs,bsn,bhpn->bshp", to_end, b_blocks, future, precision=highest)
    grad_x = intra_x + cross_x + skip_gain[None, None, :, None] * g_blocks
    cross_b = jnp.einsum("hbs,bshp,bhpn->bsn", to_end, x_blocks, future, precision=highest)
    partial_b = (intra_b + cross_b).reshape(seq_rows, state_dim)
    parts = lax.all_to_all(partial_b, HEAD, split_axis=0, concat_axis=0, tiled=True)
    b_grad = jnp.sum(parts.reshape(lax.axis_size(HEAD), -1, state_dim), axis=0)
    return (resid_grad, grad_x.reshape(seq_rows, inner_dev), b_grad)


def solution(mesh):
    seq, head = mesh.shape["seq"], mesh.shape["head"]
    levels = {getattr(d, "coords", (0, 0, 0))[2] for d in mesh.devices.flat}
    z_size = len(levels) if head % len(levels) == 0 else 1
    mesh = Mesh(mesh.devices.reshape(seq, z_size, head // z_size), DEVICES)
    return jax.shard_map(
        shards,
        mesh=mesh,
        in_specs=(
            P(DEVICES, None),
            P(DEVICES, None),
            P(DEVICES, None),
            P(DEVICES, None),
            P(DEVICES, None, None),
            P(DEVICES, None, None),
            P(DEVICES, None, None),
            P(HEAD, None),
            P("seq", HEAD),
            P("seq", None),
            P("seq", None),
            P(HEAD, "seq"),
            P(HEAD),
        ),
        out_specs=(P(DEVICES, None), P("seq", HEAD), P(DEVICES, None)),
        check_vma=False,
    )
```
